32 devices in a mesh: groups: 2 (over x), row: 8 (over z, y), col: 2 (over core).
Axes of the slice: x: 2, y: 2, z: 4, core: 2. Of those that a mesh axis runs over, the one named last changes fastest.
Arguments:
- prefix_states: bfloat16 [2048, 8192], P(('groups', 'col'), 'row'), parts along dimension 0, may hold values from -480 to 480
- prefix_gain: float32 [8192], P('row'), may hold values from 0.1 to 1.9
- backbone_key: bfloat16 [8192, 1024], P('row', 'col'), may hold values from -0.0625 to 0.0625
- backbone_value: bfloat16 [8192, 1024], P('row', 'col'), may hold values from -0.0625 to 0.0625
- action_states: bfloat16 [16384, 2048], P(('groups', 'row'), 'col'), parts along dimension 0, may hold values from -14 to 14
- expert_query: bfloat16 [2048, 2048], P('row', 'col'), may hold values from -0.25 to 0.25
- expert_key: bfloat16 [2048, 1024], P('row', 'col'), may hold values from -0.125 to 0.125
- expert_value: bfloat16 [2048, 1024], P('row', 'col'), may hold values from -0.125 to 0.125
- expert_out: bfloat16 [2048, 2048], P('col', 'row'), may hold values from -0.5 to 0.5
- prefix_length: int32 [16], P(('groups', 'row')), parts along dimension 0, may hold values from 32 to 128, as said below
- action_length: int32 [16], P(('groups', 'row')), parts along dimension 0, may hold values from 256 to 1024, as said below
Outputs:
- prefix_keys: bfloat16 [2048, 1024], P(('groups', 'row'), 'col'), parts along dimension 0
- prefix_values: bfloat16 [2048, 1024], P(('groups', 'row'), 'col'), parts along dimension 0
- action_out: bfloat16 [16384, 2048], P(('groups', 'row'), 'col'), parts along dimension 0
The draws below stay inside these ranges and needn't reach their ends.
There are 2 independent parts, one for each index of `groups`. The reference program is written for one: setup_inputs(seed, part) draws one part's arguments, and reference() takes and returns one part's arrays. A program takes and returns all parts, laid end to end along the dimension named above; an argument that names none is the same for every part. Nothing has to cross between parts.
Inputs may be any that keep to these rules, and one draw needn't show every extreme that they name: `prefix_length`: every draw has an episode with all 128 prefix tokens valid. `action_length`: every draw has an episode with all 1024 action tokens valid.
All inputs are finite; a program needn't handle non-finite values.
Results may differ from the reference program's by a relative error of at most 0.0095.
Values may be sent and summed in bfloat16 or wider, within the bound.
A program may use at most 128 MiB of HBM per device.

```python
import math
import jax
import jax.numpy as jnp
from jax import lax

D = 8192
KV_HEADS = 8
HEAD = 128
DA = 2048
PREF = 128
ACT = 1024
KV = 1024
QW = 2048
EPISODES = 8


def draw_prefix_states(key, part):
    row_count = EPISODES * PREF
    base_key, col_key, row_key = jax.random.split(jax.random.fold_in(key, 101), 3)
    column_trend = 3.0 ** (jnp.arange(D, dtype=jnp.float32) / D)
    jitter = jnp.exp(jax.random.uniform(col_key, (D,), minval=-1.15, maxval=1.15))
    row_scale = jnp.exp(jax.random.uniform(row_key, (row_count, 1), minval=0.0, maxval=math.log(10.0)))
    base_draw = jnp.clip(jax.random.normal(base_key, (row_count, D)), -5.0, 5.0)
    return (base_draw * (column_trend * jitter)[None, :] * row_scale).astype(jnp.bfloat16)


def draw_action_states(key, part):
    row_count = EPISODES * ACT
    draw_key = jax.random.fold_in(jax.random.fold_in(key, 202), 0)
    base_draw = jnp.clip(jax.random.normal(draw_key, (EPISODES, ACT, DA)), -4.0, 4.0)
    return base_draw.reshape(row_count, DA).astype(jnp.bfloat16)


def draw_prefix_length(key, part):
    length_key, full_key = jax.random.split(jax.random.fold_in(key, 303))
    lengths = jax.random.randint(length_key, (EPISODES,), max(PREF // 4, 1), PREF + 1)
    full_slot = jax.random.randint(full_key, (), 0, EPISODES)
    return jnp.where(jnp.arange(EPISODES) == full_slot, PREF, lengths).astype(jnp.int32)


def draw_action_length(key, part):
    length_key, full_key = jax.random.split(jax.random.fold_in(key, 404))
    lengths = jax.random.randint(length_key, (EPISODES,), max(ACT // 4, 1), ACT + 1)
    full_slot = jax.random.randint(full_key, (), 0, EPISODES)
    return jnp.where(jnp.arange(EPISODES) == full_slot, ACT, lengths).astype(jnp.int32)


def block_scale(stream_key, shape, shards, smallest, largest):
    loudness, own = 1.0, jax.random.fold_in(stream_key, 6)
    for axis_at, shards_of in shards:
        heights = jnp.exp(jax.random.uniform(jax.random.fold_in(own, axis_at), (shards_of,), jnp.float32, smallest / len(shards), largest / len(shards)))
        loudness = loudness * jnp.repeat(heights, shape[axis_at] // shards_of).reshape([-1 if axis == axis_at else 1 for axis in range(len(shape))])
    return loudness


def bell_draw(stream_key, dims, scale, limit, cuts=(), held_as=jnp.bfloat16):
    values = jax.random.normal(stream_key, dims, jnp.float32) * scale
    if len(cuts) > 0:
        values = block_scale(stream_key, dims, cuts, -0.22, 0.18) * values
    return jnp.clip(values, min=-limit, max=limit).astype(held_as)


def setup_inputs(seed: int = 0, part: int = 0) -> dict:
    seeds = jax.random.split(jax.random.key(seed), 12)
    own_keys = jax.random.split(jax.random.fold_in(seeds[11], part), 12)
    return {
        "prefix_states": draw_prefix_states(jax.random.fold_in(jax.random.fold_in(seeds[11], part), 71), part),
        "prefix_gain": jnp.clip(1.0 + 0.18 * jax.random.normal(seeds[1], (D,), jnp.float32), 0.1, 1.9),
        "backbone_key": bell_draw(seeds[2], (D, KV), D ** -0.5, 0.0625, ((0, 8), (1, 2))),
        "backbone_value": bell_draw(seeds[3], (D, KV), D ** -0.5, 0.0625, ((0, 8), (1, 2))),
        "action_states": draw_action_states(jax.random.fold_in(jax.random.fold_in(seeds[11], part), 71), part),
        "expert_query": bell_draw(seeds[5], (DA, QW), (DA // 4) ** -0.5, 0.25, ((0, 8), (1, 2))),
        "expert_key": bell_draw(seeds[6], (DA, KV), DA ** -0.5, 0.125, ((0, 8), (1, 2))),
        "expert_value": bell_draw(seeds[7], (DA, KV), DA ** -0.5, 0.125, ((0, 8), (1, 2))),
        "expert_out": bell_draw(seeds[8], (QW, DA), (QW // 16) ** -0.5, 0.5, ((0, 2), (1, 8))),
        "prefix_length": draw_prefix_length(jax.random.fold_in(jax.random.fold_in(seeds[11], part), 71), part),
        "action_length": draw_action_length(jax.random.fold_in(jax.random.fold_in(seeds[11], part), 71), part),
    }


def attend(packed):
    prefix_k, prefix_v, query_e, key_e, value_e, prefix_valid, action_valid = packed
    queries = query_e.astype(jnp.float32).reshape(ACT, KV_HEADS, 2, HEAD)
    keys_all = jnp.concatenate([prefix_k, key_e], axis=0).astype(jnp.float32).reshape(PREF + ACT, KV_HEADS, HEAD)
    values_all = jnp.concatenate([prefix_v, value_e], axis=0).astype(jnp.float32).reshape(PREF + ACT, KV_HEADS, HEAD)
    valid = jnp.concatenate([jnp.arange(PREF) < prefix_valid, jnp.arange(ACT) < action_valid])
    scores = jnp.einsum('qgjd,kgd->gjqk', queries, keys_all) * HEAD ** (-0.5)
    scores = jnp.where(valid[None, None, None, :], scores, -1e+30)
    highest = lax.optimization_barrier(jnp.max(scores, axis=-1, keepdims=True))
    exponent = jnp.exp(scores - highest)
    weights = (exponent / lax.optimization_barrier(jnp.sum(exponent, axis=-1, keepdims=True))).astype(jnp.bfloat16)
    attended = jnp.einsum('gjqk,kgd->qgjd', weights.astype(jnp.float32), values_all)
    return attended.reshape(ACT, QW).astype(jnp.bfloat16)

def reference(prefix_states, prefix_gain, backbone_key, backbone_value, action_states, expert_query, expert_key, expert_value, expert_out, prefix_length, action_length):
    states = prefix_states.astype(jnp.float32)
    squares = lax.optimization_barrier(jnp.sum(states * states, axis=1, keepdims=True))
    normed = (states * lax.rsqrt(squares / D + 1e-06) * prefix_gain[None, :]).astype(jnp.bfloat16)
    prefix_keys = jnp.dot(normed, backbone_key, preferred_element_type=jnp.float32).astype(jnp.bfloat16)
    prefix_values = jnp.dot(normed, backbone_value, preferred_element_type=jnp.float32).astype(jnp.bfloat16)
    action_query = jnp.dot(action_states, expert_query, preferred_element_type=jnp.float32).astype(jnp.bfloat16)
    action_key = jnp.dot(action_states, expert_key, preferred_element_type=jnp.float32).astype(jnp.bfloat16)
    action_value = jnp.dot(action_states, expert_value, preferred_element_type=jnp.float32).astype(jnp.bfloat16)
    packed = (prefix_keys.reshape(EPISODES, PREF, KV), prefix_values.reshape(EPISODES, PREF, KV), action_query.reshape(EPISODES, ACT, QW), action_key.reshape(EPISODES, ACT, KV), action_value.reshape(EPISODES, ACT, KV), prefix_length, action_length)
    attended = lax.map(attend, packed).reshape(EPISODES * ACT, QW)
    action_out = jnp.dot(attended, expert_out, preferred_element_type=jnp.float32).astype(jnp.bfloat16)
    return (prefix_keys, prefix_values, action_out)
```

```python
import functools
import math

import jax
import jax.numpy as jnp
import numpy as np
from jax import lax
from jax.experimental import pallas as pl
from jax.experimental.pallas import tpu as pltpu
from jax.sharding import PartitionSpec as P

HEAD = 128
F32 = jnp.float32
BF16 = jnp.bfloat16


def attend_kernel(scale, plen_ref, alen_ref, q_ref, pk_ref, ak_ref, pv_ref, av_ref, o_ref):
    nt = (((1,), (1,)), ((), ()))
    prefix_count, token_count = pk_ref.shape[0], ak_ref.shape[0]
    prefix_bias = jnp.where(
        lax.broadcasted_iota(jnp.int32, (1, prefix_count), 1) < plen_ref[0], 0.0, -1e30
    )
    action_bias = jnp.where(
        lax.broadcasted_iota(jnp.int32, (1, token_count), 1) < alen_ref[0], 0.0, -1e30
    )
    for j in range(q_ref.shape[1] // HEAD):
        cols = slice(j * HEAD, (j + 1) * HEAD)
        q = q_ref[:, cols]
        sp = lax.dot_general(q, pk_ref[...], nt, preferred_element_type=F32) + prefix_bias
        sa = lax.dot_general(q, ak_ref[...], nt, preferred_element_type=F32) + action_bias
        top = jnp.maximum(
            jnp.max(sp, axis=-1, keepdims=True), jnp.max(sa, axis=-1, keepdims=True)
        )
        ep = jnp.exp2((sp - top) * scale)
        ea = jnp.exp2((sa - top) * scale)
        total = jnp.sum(ep, axis=-1, keepdims=True) + jnp.sum(ea, axis=-1, keepdims=True)
        out = jnp.dot(ep.astype(BF16), pv_ref[...], preferred_element_type=F32)
        out += jnp.dot(ea.astype(BF16), av_ref[...], preferred_element_type=F32)
        o_ref[:, cols] = (out / total).astype(BF16)


def attend(plen, alen, query, pk, ak, pv, av):
    tokens, query_cols = query.shape
    groups = ak.shape[1] // HEAD
    width = query_cols // groups
    rows = math.gcd(tokens, 256)
    keys = pk.shape[0] + ak.shape[0]
    smem = pl.BlockSpec(memory_space=pltpu.SMEM)
    return pl.pallas_call(
        functools.partial(attend_kernel, HEAD**-0.5 * math.log2(math.e)),
        grid=(groups, tokens // rows),
        in_specs=[
            smem,
            smem,
            pl.BlockSpec((rows, width), lambda g, i: (i, g)),
            pl.BlockSpec((pk.shape[0], HEAD), lambda g, i: (0, g)),
            pl.BlockSpec((ak.shape[0], HEAD), lambda g, i: (0, g)),
            pl.BlockSpec((pv.shape[0], HEAD), lambda g, i: (0, g)),
            pl.BlockSpec((av.shape[0], HEAD), lambda g, i: (0, g)),
        ],
        out_specs=pl.BlockSpec((rows, width), lambda g, i: (i, g)),
        out_shape=jax.ShapeDtypeStruct((tokens, query_cols), BF16),
        compiler_params=pltpu.CompilerParams(vmem_limit_bytes=32 * 1024 * 1024),
        cost_estimate=pl.CostEstimate(
            flops=8 * tokens * query_cols * keys,
            bytes_accessed=4 * tokens * query_cols,
            transcendentals=tokens * keys * query_cols // HEAD,
        ),
        name="attend",
    )(plen, alen, query, pk, ak, pv, av)


def shards(
    mesh,
    prefix_states,
    prefix_gain,
    backbone_key,
    backbone_value,
    action_states,
    expert_query,
    expert_key,
    expert_value,
    expert_out,
    prefix_length,
    action_length,
):
    count = mesh.shape["row"]
    ring = list(range(0, count, 2)) + list(range(count - 1, 0, -2))
    place = np.argsort(np.array(ring))
    shifts = np.array(
        [[ring[(place[r] + s) % count] for s in range(count)] for r in range(count)], np.uint32
    )
    ahead = [(ring[p], ring[(p + 1) % count]) for p in range(count)]
    back = [(b, a) for a, b in ahead]
    mine = lax.axis_index("row").astype(jnp.uint32)
    zero = jnp.uint32(0)
    shifted = lax.dynamic_slice(jnp.array(shifts), (mine, zero), (1, count))
    col = lax.axis_index("col").astype(jnp.uint32)
    swap = [(0, 1), (1, 0)]

    def row_at(shift):
        return shifted[0, shift % count]

    def cut(array, start, size, axis):
        begin = (start, zero) if axis == 0 else (zero, start)
        sizes = (size, array.shape[1]) if axis == 0 else (array.shape[0], size)
        return lax.dynamic_slice(array, begin, sizes)

    def gather(block):
        got = []
        ahead_block = back_block = block
        for step in range(1, count // 2):
            ahead_block = lax.ppermute(ahead_block, "row", ahead)
            back_block = lax.ppermute(back_block, "row", back)
            got.append((row_at(-step), ahead_block, row_at(step), back_block))
        half = block.shape[0] // 2
        last = jnp.concatenate(
            [
                lax.ppermute(ahead_block[:half], "row", ahead),
                lax.ppermute(back_block[half:], "row", back),
            ],
            axis=0,
        )
        return got, (row_at(count // 2), last)

    def both(block, axis):
        other = lax.ppermute(block, "col", swap)
        low = jnp.where(col == 0, block, other)
        high = jnp.where(col == 0, other, block)
        return jnp.concatenate([low, high], axis=axis)

    joined = jnp.concatenate([expert_query, expert_key, expert_value], axis=1)
    weight_pairs, weight_last = gather(joined)

    states = both(prefix_states, 0)
    wide = states.astype(F32)
    squares = jnp.sum(wide * wide, axis=1)
    features = prefix_states.shape[1] * count
    all_squares = lax.all_gather(squares, "row", axis=0)
    scaled = (wide * prefix_gain[None, :]).astype(BF16)
    key_part = jnp.dot(scaled, backbone_key, preferred_element_type=F32)
    value_part = jnp.dot(scaled, backbone_value, preferred_element_type=F32)
    own = states.shape[0] // count

    def part(array, row):
        return cut(array, row * own, own, 0)

    key_run = part(key_part, row_at(-1))
    value_run = part(value_part, row_at(1))
    for step in range(count - 1):
        key_run = lax.ppermute(key_run.astype(BF16), "row", ahead).astype(F32)
        value_run = lax.ppermute(value_run.astype(BF16), "row", back).astype(F32)
        key_run += part(key_part, row_at(-2 - step))
        value_run += part(value_part, row_at(2 + step - count))
    own_squares = lax.dynamic_slice(jnp.sum(all_squares, axis=0), (mine * own,), (own,))
    row_scale = lax.rsqrt(own_squares / features + 1e-06)[:, None]
    prefix_keys = (key_run * row_scale).astype(BF16)
    prefix_values = (value_run * row_scale).astype(BF16)

    actions = both(action_states, 1)
    depth = joined.shape[0]

    def columns(row):
        return cut(actions, row * depth, depth, 1)

    total = jnp.dot(columns(mine), joined, preferred_element_type=F32)
    for row_a, block_a, row_b, block_b in weight_pairs:
        total += jnp.dot(
            jnp.concatenate([columns(row_a), columns(row_b)], axis=1),
            jnp.concatenate([block_a, block_b], axis=0),
            preferred_element_type=F32,
        )
    row_c, block_c = weight_last
    total += jnp.dot(columns(row_c), block_c, preferred_element_type=F32)
    projected = total.astype(BF16)
    query_cols, key_cols = expert_query.shape[1], expert_key.shape[1]
    query = projected[:, :query_cols]
    action_key = projected[:, query_cols : query_cols + key_cols]
    action_value = projected[:, query_cols + key_cols :]

    later, _ = lax.optimization_barrier((expert_out, block_c))
    out_pairs, out_last = gather(later)
    piece = expert_out.shape[1]
    out_weight = jnp.zeros((expert_out.shape[0], piece * count), BF16)
    placed = [(mine, expert_out)]
    for row_a, block_a, row_b, block_b in out_pairs:
        placed += [(row_a, block_a), (row_b, block_b)]
    placed.append(out_last)
    for row, block in placed:
        out_weight = lax.dynamic_update_slice(out_weight, block, (zero, row * piece))

    attended = attend(
        prefix_length, action_length, query, prefix_keys, action_key, prefix_values, action_value
    )
    half = out_weight.shape[1] // 2

    def product(which):
        weight = cut(out_weight, which * half, half, 1)
        return jnp.dot(attended, weight, preferred_element_type=F32)

    sent = lax.ppermute(product(1 - col).astype(BF16), "col", swap)
    action_out = (product(col) + sent.astype(F32)).astype(BF16)
    return (prefix_keys, prefix_values, action_out)


def solution(mesh):
    placed = (
        P(("groups", "col"), "row"),
        P("row"),
        P("row", "col"),
        P("row", "col"),
        P(("groups", "row"), "col"),
        P("row", "col"),
        P("row", "col"),
        P("row", "col"),
        P("col", "row"),
        P(("groups", "row")),
        P(("groups", "row")),
    )
    return jax.shard_map(
        functools.partial(shards, mesh),
        mesh=mesh,
        in_specs=placed,
        out_specs=(
            P(("groups", "row"), "col"),
            P(("groups", "row"), "col"),
            P(("groups", "row"), "col"),
        ),
        check_vma=False,
    )
```

```python
import functools
import math

import jax
import jax.numpy as jnp
import numpy as np
from jax import lax
from jax.experimental import pallas as pl
from jax.experimental.pallas import tpu as pltpu
from jax.sharding import PartitionSpec as P

HEAD = 128
F32 = jnp.float32
BF16 = jnp.bfloat16


def attend_kernel(scale, plen_ref, alen_ref, q_ref, pk_ref, ak_ref, pv_ref, av_ref, o_ref):
    nt = (((1,), (1,)), ((), ()))
    prefix_count, token_count = pk_ref.shape[0], ak_ref.shape[0]
    prefix_bias = jnp.where(
        lax.broadcasted_iota(jnp.int32, (1, prefix_count), 1) < plen_ref[0], 0.0, -1e30
    )
    action_bias = jnp.where(
        lax.broadcasted_iota(jnp.int32, (1, token_count), 1) < alen_ref[0], 0.0, -1e30
    )
    for j in range(q_ref.shape[1] // HEAD):
        cols = slice(j * HEAD, (j + 1) * HEAD)
        q = q_ref[:, cols]
        sp = lax.dot_general(q, pk_ref[...], nt, preferred_element_type=F32) + prefix_bias
        sa = lax.dot_general(q, ak_ref[...], nt, preferred_element_type=F32) + action_bias
        top = jnp.maximum(
            jnp.max(sp, axis=-1, keepdims=True), jnp.max(sa, axis=-1, keepdims=True)
        )
        ep = jnp.exp2((sp - top) * scale)
        ea = jnp.exp2((sa - top) * scale)
        total = jnp.sum(ep, axis=-1, keepdims=True) + jnp.sum(ea, axis=-1, keepdims=True)
        out = jnp.dot(ep.astype(BF16), pv_ref[...], preferred_element_type=F32)
        out += jnp.dot(ea.astype(BF16), av_ref[...], preferred_element_type=F32)
        o_ref[:, cols] = (out / total).astype(BF16)


def attend(plen, alen, query, pk, ak, pv, av):
    tokens, query_cols = query.shape
    groups = ak.shape[1] // HEAD
    width = query_cols // groups
    rows = math.gcd(tokens, 256)
    keys = pk.shape[0] + ak.shape[0]
    smem = pl.BlockSpec(memory_space=pltpu.SMEM)
    return pl.pallas_call(
        functools.partial(attend_kernel, HEAD**-0.5 * math.log2(math.e)),
        grid=(groups, tokens // rows),
        in_specs=[
            smem,
            smem,
            pl.BlockSpec((rows, width), lambda g, i: (i, g)),
            pl.BlockSpec((pk.shape[0], HEAD), lambda g, i: (0, g)),
            pl.BlockSpec((ak.shape[0], HEAD), lambda g, i: (0, g)),
            pl.BlockSpec((pv.shape[0], HEAD), lambda g, i: (0, g)),
            pl.BlockSpec((av.shape[0], HEAD), lambda g, i: (0, g)),
        ],
        out_specs=pl.BlockSpec((rows, width), lambda g, i: (i, g)),
        out_shape=jax.ShapeDtypeStruct((tokens, query_cols), BF16),
        compiler_params=pltpu.CompilerParams(vmem_limit_bytes=32 * 1024 * 1024),
        cost_estimate=pl.CostEstimate(
            flops=8 * tokens * query_cols * keys,
            bytes_accessed=4 * tokens * query_cols,
            transcendentals=tokens * keys * query_cols // HEAD,
        ),
        name="attend",
    )(plen, alen, query, pk, ak, pv, av)


def shards(
    mesh,
    prefix_states,
    prefix_gain,
    backbone_key,
    backbone_value,
    action_states,
    expert_query,
    expert_key,
    expert_value,
    expert_out,
    prefix_length,
    action_length,
):
    count = mesh.shape["row"]
    ring = list(range(0, count, 2)) + list(range(count - 1, 0, -2))
    place = np.argsort(np.array(ring))
    shifts = np.array(
        [[ring[(place[r] + s) % count] for s in range(count)] for r in range(count)], np.uint32
    )
    ahead = [(ring[p], ring[(p + 1) % count]) for p in range(count)]
    back = [(b, a) for a, b in ahead]
    mine = lax.axis_index("row").astype(jnp.uint32)
    zero = jnp.uint32(0)
    shifted = lax.dynamic_slice(jnp.array(shifts), (mine, zero), (1, count))
    col = lax.axis_index("col").astype(jnp.uint32)
    swap = [(0, 1), (1, 0)]

    def row_at(shift):
        return shifted[0, shift % count]

    def cut(array, start, size, axis):
        begin = (start, zero) if axis == 0 else (zero, start)
        sizes = (size, array.shape[1]) if axis == 0 else (array.shape[0], size)
        return lax.dynamic_slice(array, begin, sizes)

    def gather(block):
        got = []
        ahead_block = back_block = block
        for step in range(1, count // 2):
            ahead_block = lax.ppermute(ahead_block, "row", ahead)
            back_block = lax.ppermute(back_block, "row", back)
            got.append((row_at(-step), ahead_block, row_at(step), back_block))
        half = block.shape[0] // 2
        last = jnp.concatenate(
            [
                lax.ppermute(ahead_block[:half], "row", ahead),
                lax.ppermute(back_block[half:], "row", back),
            ],
            axis=0,
        )
        return got, (row_at(count // 2), last)

    def both(block, axis):
        other = lax.ppermute(block, "col", swap)
        low = jnp.where(col == 0, block, other)
        high = jnp.where(col == 0, other, block)
        return jnp.concatenate([low, high], axis=axis)

    joined = jnp.concatenate([expert_query, expert_key, expert_value], axis=1)
    weight_pairs, weight_last = gather(joined)

    states = both(prefix_states, 0)
    wide = states.astype(F32)
    squares = jnp.sum(wide * wide, axis=1)
    features = prefix_states.shape[1] * count
    if count & (count - 1):
        squares = lax.psum(squares, "row")
    else:
        hop = 1
        while hop < count:
            pairs = [(r, r ^ hop) for r in range(count)]
            squares += lax.ppermute(squares, "row", pairs)
            hop *= 2
    scaled = (wide * prefix_gain[None, :]).astype(BF16)
    key_part = jnp.dot(scaled, backbone_key, preferred_element_type=F32)
    value_part = jnp.dot(scaled, backbone_value, preferred_element_type=F32)
    own = states.shape[0] // count

    def part(array, row):
        return cut(array, row * own, own, 0)

    key_run = part(key_part, row_at(-1))
    value_run = part(value_part, row_at(1))
    for step in range(count - 1):
        if step == 2 and len(weight_pairs) > 2:
            key_run, value_run, _, _ = lax.optimization_barrier(
                (key_run, value_run, weight_pairs[1][1], weight_pairs[1][3])
            )
        key_run = lax.ppermute(key_run.astype(BF16), "row", ahead).astype(F32)
        value_run = lax.ppermute(value_run.astype(BF16), "row", back).astype(F32)
        key_run += part(key_part, row_at(-2 - step))
        value_run += part(value_part, row_at(2 + step - count))
    own_squares = lax.dynamic_slice(squares, (mine * own,), (own,))
    row_scale = lax.rsqrt(own_squares / features + 1e-06)[:, None]
    prefix_keys = (key_run * row_scale).astype(BF16)
    prefix_values = (value_run * row_scale).astype(BF16)

    action_states, states = lax.optimization_barrier((action_states, states))
    actions = both(action_states, 1)
    depth = joined.shape[0]

    def columns(row):
        return cut(actions, row * depth, depth, 1)

    row_c, block_c = weight_last
    blocks = [(mine, joined)]
    for row_a, block_a, row_b, block_b in weight_pairs:
        blocks += [(row_a, block_a), (row_b, block_b)]
    blocks.append((row_c, block_c))
    early = max(1, len(blocks) - 3)

    def product_of(some):
        return jnp.dot(
            jnp.concatenate([columns(row) for row, _ in some], axis=1),
            jnp.concatenate([block for _, block in some], axis=0),
            preferred_element_type=F32,
        )

    total = lax.optimization_barrier(product_of(blocks[:early])) + product_of(blocks[early:])
    projected = total.astype(BF16)
    query_cols, key_cols = expert_query.shape[1], expert_key.shape[1]
    query = projected[:, :query_cols]
    action_key = projected[:, query_cols : query_cols + key_cols]
    action_value = projected[:, query_cols + key_cols :]

    later, _ = lax.optimization_barrier((expert_out, block_c))
    out_pairs, out_last = gather(later)
    piece = expert_out.shape[1]
    out_weight = jnp.zeros((expert_out.shape[0], piece * count), BF16)
    placed = [(mine, expert_out)]
    for row_a, block_a, row_b, block_b in out_pairs:
        placed += [(row_a, block_a), (row_b, block_b)]
    placed.append(out_last)
    for row, block in placed:
        out_weight = lax.dynamic_update_slice(out_weight, block, (zero, row * piece))

    attended = attend(
        prefix_length, action_length, query, prefix_keys, action_key, prefix_values, action_value
    )
    half = out_weight.shape[1] // 2

    def product(which):
        weight = cut(out_weight, which * half, half, 1)
        return jnp.dot(attended, weight, preferred_element_type=F32)

    away = product(1 - col).astype(BF16)
    sent = lax.ppermute(away, "col", swap)
    kept = lax.optimization_barrier(product(col))
    action_out = (kept + sent.astype(F32)).astype(BF16)
    return (prefix_keys, prefix_values, action_out)


def solution(mesh):
    placed = (
        P(("groups", "col"), "row"),
        P("row"),
        P("row", "col"),
        P("row", "col"),
        P(("groups", "row"), "col"),
        P("row", "col"),
        P("row", "col"),
        P("row", "col"),
        P("col", "row"),
        P(("groups", "row")),
        P(("groups", "row")),
    )
    return jax.shard_map(
        functools.partial(shards, mesh),
        mesh=mesh,
        in_specs=placed,
        out_specs=(
            P(("groups", "row"), "col"),
            P(("groups", "row"), "col"),
            P(("groups", "row"), "col"),
        ),
        check_vma=False,
    )
```

```python
import functools
import math

import jax
import jax.numpy as jnp
import numpy as np
from jax import lax
from jax.experimental import pallas as pl
from jax.experimental.pallas import tpu as pltpu
from jax.sharding import PartitionSpec as P

HEAD = 128
F32 = jnp.float32
BF16 = jnp.bfloat16


def attend_kernel(scale, plen_ref, alen_ref, q_ref, pk_ref, ak_ref, pv_ref, av_ref, o_ref):
    nt = (((1,), (1,)), ((), ()))
    prefix_count, token_count = pk_ref.shape[0], ak_ref.shape[0]
    prefix_bias = jnp.where(
        lax.broadcasted_iota(jnp.int32, (1, prefix_count), 1) < plen_ref[0], 0.0, -1e30
    )
    action_bias = jnp.where(
        lax.broadcasted_iota(jnp.int32, (1, token_count), 1) < alen_ref[0], 0.0, -1e30
    )
    for j in range(q_ref.shape[1] // HEAD):
        cols = slice(j * HEAD, (j + 1) * HEAD)
        q = q_ref[:, cols]
        sp = lax.dot_general(q, pk_ref[...], nt, preferred_element_type=F32) + prefix_bias
        sa = lax.dot_general(q, ak_ref[...], nt, preferred_element_type=F32) + action_bias
        top = jnp.maximum(
            jnp.max(sp, axis=-1, keepdims=True), jnp.max(sa, axis=-1, keepdims=True)
        )
        ep = jnp.exp2((sp - top) * scale)
        ea = jnp.exp2((sa - top) * scale)
        total = jnp.sum(ep, axis=-1, keepdims=True) + jnp.sum(ea, axis=-1, keepdims=True)
        out = jnp.dot(ep.astype(BF16), pv_ref[...], preferred_element_type=F32)
        out += jnp.dot(ea.astype(BF16), av_ref[...], preferred_element_type=F32)
        o_ref[:, cols] = (out / total).astype(BF16)


def attend(plen, alen, query, pk, ak, pv, av):
    tokens, query_cols = query.shape
    groups = ak.shape[1] // HEAD
    width = query_cols // groups
    rows = math.gcd(tokens, 256)
    keys = pk.shape[0] + ak.shape[0]
    smem = pl.BlockSpec(memory_space=pltpu.SMEM)
    return pl.pallas_call(
        functools.partial(attend_kernel, HEAD**-0.5 * math.log2(math.e)),
        grid=(groups, tokens // rows),
        in_specs=[
            smem,
            smem,
            pl.BlockSpec((rows, width), lambda g, i: (i, g)),
            pl.BlockSpec((pk.shape[0], HEAD), lambda g, i: (0, g)),
            pl.BlockSpec((ak.shape[0], HEAD), lambda g, i: (0, g)),
            pl.BlockSpec((pv.shape[0], HEAD), lambda g, i: (0, g)),
            pl.BlockSpec((av.shape[0], HEAD), lambda g, i: (0, g)),
        ],
        out_specs=pl.BlockSpec((rows, width), lambda g, i: (i, g)),
        out_shape=jax.ShapeDtypeStruct((tokens, query_cols), BF16),
        compiler_params=pltpu.CompilerParams(vmem_limit_bytes=32 * 1024 * 1024),
        cost_estimate=pl.CostEstimate(
            flops=8 * tokens * query_cols * keys,
            bytes_accessed=4 * tokens * query_cols,
            transcendentals=tokens * keys * query_cols // HEAD,
        ),
        name="attend",
    )(plen, alen, query, pk, ak, pv, av)


def shards(
    mesh,
    prefix_states,
    prefix_gain,
    backbone_key,
    backbone_value,
    action_states,
    expert_query,
    expert_key,
    expert_value,
    expert_out,
    prefix_length,
    action_length,
):
    count = mesh.shape["row"]
    ring = list(range(0, count, 2)) + list(range(count - 1, 0, -2))
    place = np.argsort(np.array(ring))
    shifts = np.array(
        [[ring[(place[r] + s) % count] for s in range(count)] for r in range(count)], np.uint32
    )
    ahead = [(ring[p], ring[(p + 1) % count]) for p in range(count)]
    back = [(b, a) for a, b in ahead]
    mine = lax.axis_index("row").astype(jnp.uint32)
    zero = jnp.uint32(0)
    shifted = lax.dynamic_slice(jnp.array(shifts), (mine, zero), (1, count))
    col = lax.axis_index("col").astype(jnp.uint32)
    swap = [(0, 1), (1, 0)]

    def row_at(shift):
        return shifted[0, shift % count]

    def cut(array, start, size, axis):
        begin = (start, zero) if axis == 0 else (zero, start)
        sizes = (size, array.shape[1]) if axis == 0 else (array.shape[0], size)
        return lax.dynamic_slice(array, begin, sizes)

    def gather(block, gate=None):
        got = []
        ahead_block = back_block = block
        for step in range(1, count // 2):
            if step == 3 and gate is not None:
                ahead_block, back_block, gate = lax.optimization_barrier(
                    (ahead_block, back_block, gate)
                )
            ahead_block = lax.ppermute(ahead_block, "row", ahead)
            back_block = lax.ppermute(back_block, "row", back)
            got.append((row_at(-step), ahead_block, row_at(step), back_block))
        half = block.shape[0] // 2
        last = jnp.concatenate(
            [
                lax.ppermute(ahead_block[:half], "row", ahead),
                lax.ppermute(back_block[half:], "row", back),
            ],
            axis=0,
        )
        return got, (row_at(count // 2), last), gate

    def both(block, axis):
        other = lax.ppermute(block, "col", swap)
        low = jnp.where(col == 0, block, other)
        high = jnp.where(col == 0, other, block)
        return jnp.concatenate([low, high], axis=axis)

    joined = jnp.concatenate([expert_query, expert_key, expert_value], axis=1)
    states = both(prefix_states, 0)
    states, action_states = lax.optimization_barrier((states, action_states))
    wide = states.astype(F32)
    squares = jnp.sum(wide * wide, axis=1)
    features = prefix_states.shape[1] * count
    scaled = (wide * prefix_gain[None, :]).astype(BF16)
    key_part = jnp.dot(scaled, backbone_key, preferred_element_type=F32)
    value_part = jnp.dot(scaled, backbone_value, preferred_element_type=F32)
    own = states.shape[0] // count

    def part(array, row):
        return cut(array, row * own, own, 0)

    key_run = part(key_part, row_at(-1))
    value_run = part(value_part, row_at(1))
    doubling = count & (count - 1) == 0
    if not doubling:
        squares = lax.psum(squares, "row")
    for step in range(count - 1):
        key_run, value_run = key_run.astype(BF16), value_run.astype(BF16)
        if doubling and 1 << step < count:
            key_run, value_run, squares = lax.optimization_barrier((key_run, value_run, squares))
            pairs = [(r, r ^ (1 << step)) for r in range(count)]
            squares += lax.ppermute(squares, "row", pairs)
        key_run = lax.ppermute(key_run, "row", ahead).astype(F32)
        value_run = lax.ppermute(value_run, "row", back).astype(F32)
        key_run += part(key_part, row_at(-2 - step))
        value_run += part(value_part, row_at(2 + step - count))
    own_squares = lax.dynamic_slice(squares, (mine * own,), (own,))
    row_scale = lax.rsqrt(own_squares / features + 1e-06)[:, None]
    prefix_keys = (key_run * row_scale).astype(BF16)
    prefix_values = (value_run * row_scale).astype(BF16)

    weight_pairs, weight_last, (prefix_keys, prefix_values) = gather(
        joined, (prefix_keys, prefix_values)
    )
    actions = both(action_states, 1)
    depth = joined.shape[0]

    def columns(row):
        return cut(actions, row * depth, depth, 1)

    row_c, block_c = weight_last
    later, block_c = lax.optimization_barrier((expert_out, block_c))
    blocks = [(mine, joined)]
    for row_a, block_a, row_b, block_b in weight_pairs:
        blocks += [(row_a, block_a), (row_b, block_b)]
    blocks.append((row_c, block_c))
    early = max(1, len(blocks) - 3)

    def product_of(some):
        return jnp.dot(
            jnp.concatenate([columns(row) for row, _ in some], axis=1),
            jnp.concatenate([block for _, block in some], axis=0),
            preferred_element_type=F32,
        )

    total = lax.optimization_barrier(product_of(blocks[:early])) + product_of(blocks[early:])
    projected = total.astype(BF16)
    query_cols, key_cols = expert_query.shape[1], expert_key.shape[1]
    query = projected[:, :query_cols]
    action_key = projected[:, query_cols : query_cols + key_cols]
    action_value = projected[:, query_cols + key_cols :]

    out_pairs, out_last, _ = gather(later)
    piece = expert_out.shape[1]
    out_weight = jnp.zeros((expert_out.shape[0], piece * count), BF16)
    placed = [(mine, expert_out)]
    for row_a, block_a, row_b, block_b in out_pairs:
        placed += [(row_a, block_a), (row_b, block_b)]
    placed.append(out_last)
    for row, block in placed:
        out_weight = lax.dynamic_update_slice(out_weight, block, (zero, row * piece))

    attended = attend(
        prefix_length, action_length, query, prefix_keys, action_key, prefix_values, action_value
    )
    half = out_weight.shape[1] // 2

    def product(which):
        weight = cut(out_weight, which * half, half, 1)
        return jnp.dot(attended, weight, preferred_element_type=F32)

    away = product(1 - col).astype(BF16)
    sent = lax.ppermute(away, "col", swap)
    kept = lax.optimization_barrier(product(col))
    action_out = (kept + sent.astype(F32)).astype(BF16)
    return (prefix_keys, prefix_values, action_out)


def solution(mesh):
    placed = (
        P(("groups", "col"), "row"),
        P("row"),
        P("row", "col"),
        P("row", "col"),
        P(("groups", "row"), "col"),
        P("row", "col"),
        P("row", "col"),
        P("row", "col"),
        P("col", "row"),
        P(("groups", "row")),
        P(("groups", "row")),
    )
    return jax.shard_map(
        functools.partial(shards, mesh),
        mesh=mesh,
        in_specs=placed,
        out_specs=(
            P(("groups", "row"), "col"),
            P(("groups", "row"), "col"),
            P(("groups", "row"), "col"),
        ),
        check_vma=False,
    )
```

```python
import functools
import math

import jax
import jax.numpy as jnp
import numpy as np
from jax import lax
from jax.experimental import pallas as pl
from jax.experimental.pallas import tpu as pltpu
from jax.sharding import PartitionSpec as P

HEAD = 128
F32 = jnp.float32
BF16 = jnp.bfloat16


def attend_kernel(scale, plen_ref, alen_ref, q_ref, pk_ref, ak_ref, pv_ref, av_ref, o_ref):
    nt = (((1,), (1,)), ((), ()))
    prefix_count, token_count = pk_ref.shape[0], ak_ref.shape[0]
    prefix_bias = jnp.where(
        lax.broadcasted_iota(jnp.int32, (1, prefix_count), 1) < plen_ref[0], 0.0, -1e30
    )
    action_bias = jnp.where(
        lax.broadcasted_iota(jnp.int32, (1, token_count), 1) < alen_ref[0], 0.0, -1e30
    )
    for j in range(q_ref.shape[1] // HEAD):
        cols = slice(j * HEAD, (j + 1) * HEAD)
        q = q_ref[:, cols]
        sp = lax.dot_general(q, pk_ref[...], nt, preferred_element_type=F32) + prefix_bias
        sa = lax.dot_general(q, ak_ref[...], nt, preferred_element_type=F32) + action_bias
        top = jnp.maximum(
            jnp.max(sp, axis=-1, keepdims=True), jnp.max(sa, axis=-1, keepdims=True)
        )
        ep = jnp.exp2((sp - top) * scale)
        ea = jnp.exp2((sa - top) * scale)
        total = jnp.sum(ep, axis=-1, keepdims=True) + jnp.sum(ea, axis=-1, keepdims=True)
        out = jnp.dot(ep.astype(BF16), pv_ref[...], preferred_element_type=F32)
        out += jnp.dot(ea.astype(BF16), av_ref[...], preferred_element_type=F32)
        o_ref[:, cols] = (out / total).astype(BF16)


def attend(plen, alen, query, pk, ak, pv, av):
    tokens, query_cols = query.shape
    groups = ak.shape[1] // HEAD
    width = query_cols // groups
    rows = math.gcd(tokens, 256)
    keys = pk.shape[0] + ak.shape[0]
    smem = pl.BlockSpec(memory_space=pltpu.SMEM)
    return pl.pallas_call(
        functools.partial(attend_kernel, HEAD**-0.5 * math.log2(math.e)),
        grid=(groups, tokens // rows),
        in_specs=[
            smem,
            smem,
            pl.BlockSpec((rows, width), lambda g, i: (i, g)),
            pl.BlockSpec((pk.shape[0], HEAD), lambda g, i: (0, g)),
            pl.BlockSpec((ak.shape[0], HEAD), lambda g, i: (0, g)),
            pl.BlockSpec((pv.shape[0], HEAD), lambda g, i: (0, g)),
            pl.BlockSpec((av.shape[0], HEAD), lambda g, i: (0, g)),
        ],
        out_specs=pl.BlockSpec((rows, width), lambda g, i: (i, g)),
        out_shape=jax.ShapeDtypeStruct((tokens, query_cols), BF16),
        compiler_params=pltpu.CompilerParams(vmem_limit_bytes=32 * 1024 * 1024),
        cost_estimate=pl.CostEstimate(
            flops=8 * tokens * query_cols * keys,
            bytes_accessed=4 * tokens * query_cols,
            transcendentals=tokens * keys * query_cols // HEAD,
        ),
        name="attend",
    )(plen, alen, query, pk, ak, pv, av)


def shards(
    mesh,
    prefix_states,
    prefix_gain,
    backbone_key,
    backbone_value,
    action_states,
    expert_query,
    expert_key,
    expert_value,
    expert_out,
    prefix_length,
    action_length,
):
    count = mesh.shape["row"]
    ring = list(range(0, count, 2)) + list(range(count - 1, 0, -2))
    place = np.argsort(np.array(ring))
    shifts = np.array(
        [[ring[(place[r] + s) % count] for s in range(count)] for r in range(count)], np.uint32
    )
    ahead = [(ring[p], ring[(p + 1) % count]) for p in range(count)]
    back = [(b, a) for a, b in ahead]
    mine = lax.axis_index("row").astype(jnp.uint32)
    zero = jnp.uint32(0)
    shifted = lax.dynamic_slice(jnp.array(shifts), (mine, zero), (1, count))
    col = lax.axis_index("col").astype(jnp.uint32)
    swap = [(0, 1), (1, 0)]

    def row_at(shift):
        return shifted[0, shift % count]

    def cut(array, start, size, axis):
        begin = (start, zero) if axis == 0 else (zero, start)
        sizes = (size, array.shape[1]) if axis == 0 else (array.shape[0], size)
        return lax.dynamic_slice(array, begin, sizes)

    def gather(block):
        got = []
        ahead_block = back_block = block
        for step in range(1, count // 2):
            ahead_block = lax.ppermute(ahead_block, "row", ahead)
            back_block = lax.ppermute(back_block, "row", back)
            got.append((row_at(-step), ahead_block, row_at(step), back_block))
        half = block.shape[0] // 2
        last = jnp.concatenate(
            [
                lax.ppermute(ahead_block[:half], "row", ahead),
                lax.ppermute(back_block[half:], "row", back),
            ],
            axis=0,
        )
        return got, (row_at(count // 2), last)

    def both(block, axis):
        other = lax.ppermute(block, "col", swap)
        low = jnp.where(col == 0, block, other)
        high = jnp.where(col == 0, other, block)
        return jnp.concatenate([low, high], axis=axis)

    joined = jnp.concatenate([expert_query, expert_key, expert_value], axis=1)
    states = both(prefix_states, 0)
    states, action_states = lax.optimization_barrier((states, action_states))
    wide = states.astype(F32)
    squares = jnp.sum(wide * wide, axis=1)
    features = prefix_states.shape[1] * count
    scaled = (wide * prefix_gain[None, :]).astype(BF16)
    key_part = jnp.dot(scaled, backbone_key, preferred_element_type=F32)
    value_part = jnp.dot(scaled, backbone_value, preferred_element_type=F32)
    own = states.shape[0] // count

    high = lax.reduce_precision(squares, 8, 7)
    middle = lax.reduce_precision(squares - high, 8, 7)
    terms = jnp.stack([high, middle, squares - high - middle], axis=1)
    terms = jnp.pad(terms, ((0, 0), (0, HEAD - terms.shape[1])))
    share = jnp.concatenate([key_part, value_part, terms], axis=1)
    outgoing = share.astype(BF16)
    received = []
    for step in range(1, count):
        pairs = [(ring[p], ring[(p + step) % count]) for p in range(count)]
        received.append(lax.ppermute(cut(outgoing, row_at(step) * own, own, 0), "row", pairs))

    weight_pairs, weight_last = gather(joined)
    if len(weight_pairs) > 1:
        row_a, block_a, row_b, block_b = weight_pairs[1]
        received, block_a, block_b = lax.optimization_barrier((received, block_a, block_b))
        weight_pairs[1] = (row_a, block_a, row_b, block_b)
    summed = cut(share, mine * own, own, 0)
    for block in received:
        summed += block.astype(F32)
    key_cols = backbone_key.shape[1]
    sums_end = 2 * key_cols
    own_squares = jnp.sum(summed[:, sums_end : sums_end + 3], axis=1, keepdims=True)
    row_scale = lax.rsqrt(own_squares / features + 1e-06)
    prefix_keys = (summed[:, :key_cols] * row_scale).astype(BF16)
    prefix_values = (summed[:, key_cols:sums_end] * row_scale).astype(BF16)

    actions = both(action_states, 1)
    depth = joined.shape[0]

    def columns(row):
        return cut(actions, row * depth, depth, 1)

    row_c, block_c = weight_last
    later, block_c = lax.optimization_barrier((expert_out, block_c))
    blocks = [(mine, joined)]
    for row_a, block_a, row_b, block_b in weight_pairs:
        blocks += [(row_a, block_a), (row_b, block_b)]
    blocks.append((row_c, block_c))
    early = max(1, len(blocks) - 3)

    def product_of(some):
        return jnp.dot(
            jnp.concatenate([columns(row) for row, _ in some], axis=1),
            jnp.concatenate([block for _, block in some], axis=0),
            preferred_element_type=F32,
        )

    total = lax.optimization_barrier(product_of(blocks[:early])) + product_of(blocks[early:])
    projected = total.astype(BF16)
    query_cols, key_cols = expert_query.shape[1], expert_key.shape[1]
    query = projected[:, :query_cols]
    action_key = projected[:, query_cols : query_cols + key_cols]
    action_value = projected[:, query_cols + key_cols :]

    out_pairs, out_last = gather(later)
    piece = expert_out.shape[1]
    out_weight = jnp.zeros((expert_out.shape[0], piece * count), BF16)
    placed = [(mine, expert_out)]
    for row_a, block_a, row_b, block_b in out_pairs:
        placed += [(row_a, block_a), (row_b, block_b)]
    placed.append(out_last)
    for row, block in placed:
        out_weight = lax.dynamic_update_slice(out_weight, block, (zero, row * piece))

    attended = attend(
        prefix_length, action_length, query, prefix_keys, action_key, prefix_values, action_value
    )
    half = out_weight.shape[1] // 2

    def product(which):
        weight = cut(out_weight, which * half, half, 1)
        return jnp.dot(attended, weight, preferred_element_type=F32)

    away = product(1 - col).astype(BF16)
    sent = lax.ppermute(away, "col", swap)
    kept = lax.optimization_barrier(product(col))
    action_out = (kept + sent.astype(F32)).astype(BF16)
    return (prefix_keys, prefix_values, action_out)


def solution(mesh):
    placed = (
        P(("groups", "col"), "row"),
        P("row"),
        P("row", "col"),
        P("row", "col"),
        P(("groups", "row"), "col"),
        P("row", "col"),
        P("row", "col"),
        P("row", "col"),
        P("col", "row"),
        P(("groups", "row")),
        P(("groups", "row")),
    )
    return jax.shard_map(
        functools.partial(shards, mesh),
        mesh=mesh,
        in_specs=placed,
        out_specs=(
            P(("groups", "row"), "col"),
            P(("groups", "row"), "col"),
            P(("groups", "row"), "col"),
        ),
        check_vma=False,
    )
```
